32 devices in a mesh: px: 8 (over y, x, core), py: 4 (over z).
Axes of the slice: x: 2, y: 2, z: 4, core: 2. Of those that a mesh axis runs over, the one named last changes fastest.
Arguments:
- node_features: bfloat16 [16384, 192], P(('px', 'py')), may hold values from -6 to 6
- edge_source: int32 [32, 3072], P(('px', 'py')), may hold values from 0 to 767
- edge_target: int32 [32, 3072], P(('px', 'py')), may hold values from 0 to 512, as said below
- halo_send: int32 [32, 64], P(('px', 'py')), may hold values from 0 to 511
- edge_weight_in: bfloat16 [384, 192], replicated, may hold values from -0.3125 to 0.3125
- edge_bias: float32 [192], replicated, may hold values from -4 to 4
- edge_weight_out: bfloat16 [192, 192], replicated, may hold values from -0.4375 to 0.4375
- node_weight_in: bfloat16 [384, 192], replicated, may hold values from -0.3125 to 0.3125
- node_bias: float32 [192], replicated, may hold values from -4 to 4
- node_weight_out: bfloat16 [192, 192], replicated, may hold values from -0.4375 to 0.4375
- cluster_owner: int32 [16384, 1], P(('px', 'py')), may hold values from 0 to 3; in each aligned block of 512 rows (0 to 511, 512 to 1023, ...) at most 256 rows name the same one
- cluster_member: int32 [16384], P(('px', 'py')), may hold values from 0 to 63
- coarse_send: int32 [32, 16], P(('px', 'py')), may hold values from 0 to 63
- coarse_source: int32 [32, 384], P(('px', 'py')), may hold values from 0 to 127
- coarse_target: int32 [32, 384], P(('px', 'py')), may hold values from 0 to 64, as said below
- coarse_edge_in: bfloat16 [384, 192], replicated, may hold values from -0.3125 to 0.3125
- coarse_edge_bias: float32 [192], replicated, may hold values from -4 to 4
- coarse_edge_out: bfloat16 [192, 192], replicated, may hold values from -0.4375 to 0.4375
- coarse_node_in: bfloat16 [384, 192], replicated, may hold values from -0.3125 to 0.3125
- coarse_node_bias: float32 [192], replicated, may hold values from -4 to 4
- coarse_node_out: bfloat16 [192, 192], replicated, may hold values from -0.4375 to 0.4375
Outputs:
- node_updated: bfloat16 [16384, 192], P(('px', 'py'))
- cluster_updated: bfloat16 [2048, 192], P(('px', 'py'))
The draws below stay inside these ranges and needn't reach their ends.
Inputs may be any that keep to these rules, and one draw needn't show every extreme that they name: `edge_target`: each device's slots hold a target node of that device; padding slots hold 512 and stand only at the end of a device's list; at least three quarters of each device's slots are live and some device has no padding. `coarse_target`: each device's slots hold a target cluster of that device; padding slots hold 64 and stand only at the end of a device's list; at least three quarters of each device's slots are live and some device has no padding. `cluster_owner`: at most 256 nodes of one device have the same owner, and in every draw some device has exactly 256 nodes with one owner.
All inputs are finite; a program needn't handle non-finite values.
Results may differ from the reference program's by a relative error of at most 0.014.
Values may be sent and summed in bfloat16 or wider, within the bound.
A program may use at most 64 MiB of HBM per device.

```python
import math
import jax
import jax.numpy as jnp
import numpy as np
from jax import lax

H = 192
NODE_DEV = 512
NBLOCK = 32
NODES = 16384
CLUST_DEV = 64
CLUSTERS = 2048
EDGE_DEV = 3072
E3_DEV = 384
HALO = 64
HALO3 = 16
OWNERS = 4
CAP = 256
N_PX = 8
N_PY = 4


def padded_targets(key, lists, top_index, length):
    first_key, second_key, third_key = jax.random.split(key, 3)
    targets = jax.random.randint(first_key, (lists, length), 0, top_index, dtype=jnp.int32)
    live_count = jax.random.randint(second_key, (lists, 1), length - length // 4, length + 1, dtype=jnp.int32)
    chosen = jax.random.randint(third_key, (), 0, lists, dtype=jnp.int32)
    row_index = lax.broadcasted_iota(jnp.int32, (lists, 1), 0)
    live_count = jnp.where(row_index == chosen, length, live_count)
    position = lax.broadcasted_iota(jnp.int32, (lists, length), 1)
    return jnp.where(position < live_count, targets, top_index).astype(jnp.int32)


def draw_edge_target(key, part):
    return padded_targets(jax.random.fold_in(key, 11), NBLOCK, NODE_DEV, EDGE_DEV)


def draw_coarse_target(key, part):
    return padded_targets(jax.random.fold_in(key, 23), NBLOCK, CLUST_DEV, E3_DEV)


def with_ends(values, stream_key, least, largest):
    shape = values.shape
    place = [jax.random.randint(jax.random.fold_in(stream_key, axis), (), 0, shape[axis]) for axis in range(len(shape))]
    values = values.at[tuple(place)].set(least)
    longest = shape.index(max(shape))
    place[longest] = (place[longest] + 1) % shape[longest]
    return values.at[tuple(place)].set(largest)


def block_scale(rng, shape, cuts, smallest, high):
    factor_of = 1.0
    for dim, blocks in cuts:
        heights = jax.random.uniform(jax.random.fold_in(jax.random.fold_in(rng, 6), dim), (blocks,), jnp.float32, smallest / len(cuts), high / len(cuts))
        factor_of = factor_of * jnp.repeat(jnp.exp(heights), shape[dim] // blocks).reshape((-1,) + (1,) * (len(shape) - 1 - dim))
    return factor_of


def rank_bounds(number_of, skew):
    weights = [(1 << 20) // math.isqrt(grade ** skew) + 1 for grade in range(1, number_of + 1)]
    scale = 1 + sum(weights) // (1 << 30)
    return np.cumsum(np.array([max(1, weight // scale) for weight in weights]))


def skewed_ids(rng, dims, number_of, lean):
    grid = rank_bounds(number_of, lean)
    lot = jax.random.randint(jax.random.fold_in(rng, 1), dims, 0, int(grid[number_of - 1]))
    rank = jnp.searchsorted(jnp.asarray(grid, jnp.int32), lot, side="right")
    return jax.random.permutation(jax.random.fold_in(rng, 2), number_of)[rank].astype(jnp.int32)


def deal_out(rng, own, number, rows, amount, top, limit, skew):
    order = jax.random.permutation(rng, amount)
    packed, ordinary = shares(amount, rows * top, limit, skew, True), shares(amount, rows * top, limit, skew, False)
    places = jnp.arange(amount)

    def named(sizes, rotation):
        used = int((sizes > 0).sum())
        fixed = max(1, used // 4)
        passed = fixed + (places - fixed + rotation * (used - fixed)) % max(1, amount - fixed)
        return jnp.zeros((amount,), jnp.int32).at[order[jnp.where(places < fixed, places, passed)]].set(jnp.asarray(sizes, jnp.int32))

    sizes = jnp.where(number % 4 == 0, named(packed, number // 4), named(ordinary, number - number // 4 - 1))
    mixed = jax.random.permutation(jax.random.fold_in(own, 3), amount)
    giver, sink = mixed[0:amount // 2 * 2:2], mixed[1:amount // 2 * 2:2]
    margin = jnp.minimum(sizes[giver] - 1, limit - sizes[sink]) // 2
    margin = jnp.where((giver == order[0]) | (sink == order[0]) | (sizes[sink] == 0), 0, jnp.maximum(margin, 0))
    passed = jax.random.randint(jax.random.fold_in(own, 4), (amount // 2,), 0, 1 << 20) % (margin + 1)
    sizes = sizes.at[giver].add(-passed).at[sink].add(passed)
    members = jnp.searchsorted(jnp.cumsum(sizes), jnp.arange(rows * top), side="right").astype(jnp.int32)
    listing = members.reshape(top, rows).T
    listing = listing[jax.random.permutation(jax.random.fold_in(own, 1), rows)]
    rotation = jax.random.randint(jax.random.fold_in(own, 2), (rows, 1), 0, top)
    return jnp.take_along_axis(listing, (jnp.arange(top)[None, :] + rotation) % top, axis=1)


def shares(number_of, total, reach, skew, full):
    loads = [(1 << 20) // math.isqrt(rank ** skew) + 1 for rank in range(1, number_of + 1)]
    largest = reach if full else min(reach, max(-(-total // number_of), total * loads[0] // sum(loads)))
    least = 1 if total - largest >= number_of - 1 else 0
    given, surplus = [largest] + [least] * (number_of - 1), total - largest - least * (number_of - 1)
    while surplus > 0:
        candidates = [i for i in range(1, number_of) if given[i] < largest] or [i for i in range(1, number_of) if given[i] < reach]
        pool, remaining = sum([loads[i] for i in candidates]), surplus
        for i in candidates:
            more = min(reach - given[i], max(1, remaining * loads[i] // pool), surplus)
            given[i] = given[i] + more
            surplus = surplus - more
    return np.array(given)


def normal_values(own_key, dims, deviation, bound, shards=(), kind=jnp.bfloat16):
    values = deviation * jax.random.normal(own_key, dims, jnp.float32)
    if shards:
        values = values * block_scale(own_key, dims, shards, -0.22, 0.18)
    return jnp.clip(values, -bound, bound).astype(kind)


def setup_inputs(seed: int = 0) -> dict:
    streams_of = jax.random.split(jax.random.key(seed), 22)
    node_features = normal_values(streams_of[0], (NODES, H), 1.0, 6.0, ((0, 32),))
    edge_source = with_ends(jax.random.randint(streams_of[1], (NBLOCK, EDGE_DEV), 0, NODE_DEV + 4 * HALO), jax.random.fold_in(streams_of[1], 1), 0, (NODE_DEV + 4 * HALO) - 1).astype(jnp.int32)
    edge_target = draw_edge_target(jax.random.fold_in(streams_of[21], 71), 0)
    halo_send = with_ends(jax.random.randint(streams_of[3], (NBLOCK, HALO), 0, NODE_DEV), jax.random.fold_in(streams_of[3], 1), 0, NODE_DEV - 1).astype(jnp.int32)
    edge_weight_in = normal_values(streams_of[4], (2 * H, H), (2 * H) ** -0.5, 0.3125)
    edge_bias = normal_values(streams_of[5], (H,), 1.0, 4.0, (), jnp.float32)
    edge_weight_out = normal_values(streams_of[6], (H, H), H ** -0.5, 0.4375)
    node_weight_in = normal_values(streams_of[7], (2 * H, H), (2 * H) ** -0.5, 0.3125)
    node_bias = normal_values(streams_of[8], (H,), 1.0, 4.0, (), jnp.float32)
    node_weight_out = normal_values(streams_of[9], (H, H), H ** -0.5, 0.4375)
    cluster_owner_keys = jax.random.split(jax.random.fold_in(streams_of[10], 1), NODES // NODE_DEV)
    cluster_owner_turns = jax.random.permutation(jax.random.fold_in(streams_of[10], 3), NODES // NODE_DEV)
    cluster_owner = jax.vmap(lambda own, number: deal_out(jax.random.fold_in(streams_of[10], 2), own, number, NODE_DEV, OWNERS, 1, CAP, 1))(cluster_owner_keys, cluster_owner_turns).reshape((NODES, 1))
    cluster_member = with_ends(skewed_ids(streams_of[11], (NODES,), CLUST_DEV, 2), jax.random.fold_in(streams_of[11], 3), 0, CLUST_DEV - 1).astype(jnp.int32)
    coarse_send = with_ends(jax.random.randint(streams_of[12], (NBLOCK, HALO3), 0, CLUST_DEV), jax.random.fold_in(streams_of[12], 1), 0, CLUST_DEV - 1).astype(jnp.int32)
    coarse_source = with_ends(jax.random.randint(streams_of[13], (NBLOCK, E3_DEV), 0, CLUST_DEV + 4 * HALO3), jax.random.fold_in(streams_of[13], 1), 0, (CLUST_DEV + 4 * HALO3) - 1).astype(jnp.int32)
    coarse_target = draw_coarse_target(jax.random.fold_in(streams_of[21], 71), 0)
    coarse_edge_in = normal_values(streams_of[15], (2 * H, H), (2 * H) ** -0.5, 0.3125)
    coarse_edge_bias = normal_values(streams_of[16], (H,), 1.0, 4.0, (), jnp.float32)
    coarse_edge_out = normal_values(streams_of[17], (H, H), H ** -0.5, 0.4375)
    coarse_node_in = normal_values(streams_of[18], (2 * H, H), (2 * H) ** -0.5, 0.3125)
    coarse_node_bias = normal_values(streams_of[19], (H,), 1.0, 4.0, (), jnp.float32)
    coarse_node_out = normal_values(streams_of[20], (H, H), H ** -0.5, 0.4375)
    return dict(node_features=node_features, edge_source=edge_source, edge_target=edge_target, halo_send=halo_send, edge_weight_in=edge_weight_in, edge_bias=edge_bias, edge_weight_out=edge_weight_out, node_weight_in=node_weight_in, node_bias=node_bias, node_weight_out=node_weight_out, cluster_owner=cluster_owner, cluster_member=cluster_member, coarse_send=coarse_send, coarse_source=coarse_source, coarse_target=coarse_target, coarse_edge_in=coarse_edge_in, coarse_edge_bias=coarse_edge_bias, coarse_edge_out=coarse_edge_out, coarse_node_in=coarse_node_in, coarse_node_bias=coarse_node_bias, coarse_node_out=coarse_node_out)


def normed(values):
    center = values - lax.optimization_barrier(jnp.mean(values, axis=-1, keepdims=True))
    return center * lax.rsqrt(lax.optimization_barrier(jnp.mean(center * center, axis=-1, keepdims=True)) + 1e-05)

def neighbour_table(send, per_device, blocks):
    device = jnp.arange(blocks).astype(jnp.int32)
    first_pos = device // N_PY
    second_pos = device % N_PY
    own_ids = (device[:, None] * per_device + jnp.arange(per_device).astype(jnp.int32)[None, :]).astype(jnp.int32)
    columns_list = [own_ids]
    for offset_first, offset_second in ((-1, 0), (1, 0), (0, -1), (0, 1)):
        near_first = first_pos + offset_first
        near_second = second_pos + offset_second
        inside = (near_first >= 0) & (near_first < N_PX) & (near_second >= 0) & (near_second < N_PY)
        near_device = (jnp.clip(near_first, 0, N_PX - 1) * N_PY + jnp.clip(near_second, 0, N_PY - 1)).astype(jnp.int32)
        global_ids = (near_device[:, None] * per_device + send[near_device]).astype(jnp.int32)
        columns_list.append(jnp.where(inside[:, None], global_ids, blocks * per_device).astype(jnp.int32))
    return jnp.concatenate(columns_list, axis=1).astype(jnp.int32)

def level_round(features, sources, targets, send, per_device, weights):
    weight_in, bias, weight_out, node_in, node_bias, node_out = weights
    blocks = sources.shape[0]
    width = features.shape[1]
    lookup = neighbour_table(send, per_device, blocks)
    global_sources = jnp.take_along_axis(lookup, sources, axis=1).astype(jnp.int32)
    padded = jnp.concatenate([features, jnp.zeros((1, width), jnp.bfloat16)], axis=0)

    def one_device(pieces):
        local_rows, source_ids, target_ids = pieces
        paired = jnp.concatenate([jnp.take(padded, source_ids, axis=0), jnp.take(local_rows, jnp.minimum(target_ids, per_device - 1), axis=0)], axis=1)
        hidden = jax.nn.silu(jnp.dot(paired, weight_in, preferred_element_type=jnp.float32) + bias).astype(jnp.bfloat16)
        message = normed(jnp.dot(hidden, weight_out, preferred_element_type=jnp.float32))
        totals = jnp.zeros((per_device, width), jnp.float32).at[target_ids].add(message, mode='drop')
        joined = jnp.concatenate([local_rows, totals.astype(jnp.bfloat16)], axis=1)
        node_hidden = jax.nn.silu(jnp.dot(joined, node_in, preferred_element_type=jnp.float32) + node_bias).astype(jnp.bfloat16)
        return (local_rows.astype(jnp.float32) + normed(jnp.dot(node_hidden, node_out, preferred_element_type=jnp.float32))).astype(jnp.bfloat16)
    result = lax.map(one_device, (features.reshape(blocks, per_device, width), global_sources, targets))
    return result.reshape(features.shape)

def reference(node_features, edge_source, edge_target, halo_send, edge_weight_in, edge_bias, edge_weight_out, node_weight_in, node_bias, node_weight_out, cluster_owner, cluster_member, coarse_send, coarse_source, coarse_target, coarse_edge_in, coarse_edge_bias, coarse_edge_out, coarse_node_in, coarse_node_bias, coarse_node_out):
    node_updated = level_round(node_features, edge_source, edge_target, halo_send, NODE_DEV, (edge_weight_in, edge_bias, edge_weight_out, node_weight_in, node_bias, node_weight_out))
    device = (jnp.arange(NODES) // NODE_DEV).astype(jnp.int32)
    position = ((device // N_PY * N_PY + cluster_owner[:, 0]) * CLUST_DEV + cluster_member).astype(jnp.int32)
    pooled = jax.ops.segment_sum(node_updated.astype(jnp.float32), position, num_segments=CLUSTERS)
    counts = jax.ops.segment_sum(jnp.ones((NODES,), jnp.float32), position, num_segments=CLUSTERS)
    coarse = (pooled / jnp.maximum(counts, 1.0)[:, None]).astype(jnp.bfloat16)
    cluster_updated = level_round(coarse, coarse_source, coarse_target, coarse_send, CLUST_DEV, (coarse_edge_in, coarse_edge_bias, coarse_edge_out, coarse_node_in, coarse_node_bias, coarse_node_out))
    return (node_updated, cluster_updated)
```

```python
import functools
import math

import jax
import jax.numpy as jnp
from jax import lax
from jax.experimental import pallas as pl
from jax.experimental.pallas import tpu as pltpu
from jax.sharding import PartitionSpec as P

CLUST_DEV = 64
BF = jnp.bfloat16
F32 = jnp.float32
MESH = pl.DeviceIdType.MESH


def dot(a, b):
    return jnp.dot(a, b, preferred_element_type=F32)


def dot_nt(a, b):
    return lax.dot_general(a, b, (((1,), (1,)), ((), ())), preferred_element_type=F32)


def silu(x):
    half = 0.5 * x
    return half + half * jnp.tanh(half)


def normed(v, axis):
    scale = 1.0 / v.shape[axis]
    center = v - jnp.sum(v, axis=axis, keepdims=True) * scale
    var = jnp.sum(center * center, axis=axis, keepdims=True) * scale
    return center * lax.rsqrt(var + 1e-05)


def one_hot_columns(ids, first, count):
    rows = lax.broadcasted_iota(jnp.int32, (count, ids.shape[1]), 0)
    return jnp.where(rows == ids - first, 1.0, 0.0).astype(BF)


def column(ref):
    return jnp.broadcast_to(ref[...], (8, ref.shape[1])).T[:, :1]


def flip(ref):
    return ref[...].astype(F32).T.astype(BF)


def node_part(feats, incoming, in_ref, bias_ref, out_ref):
    joined = jnp.concatenate([feats, incoming], axis=0)
    hidden = silu(dot(in_ref[...], joined) + column(bias_ref)).astype(BF)
    return (feats.astype(F32) + normed(dot(flip(out_ref), hidden), 0)).astype(BF)


def kernel(
    n_px, n_py, chunk,
    feats_ref, src_ref, tgt_ref, send_ref, ew_ref, eb_ref, eo_ref, nw_ref, nb_ref, no_ref,
    owner_ref, member_ref, csend_ref, csrc_ref, ctgt_ref, cew_ref, ceb_ref, ceo_ref,
    cnw_ref, cnb_ref, cno_ref,
    out_ref, cout_ref,
    halo_out, halo_in, chalo_out, chalo_in, pool_out, pool_in, aug,
    at_own, bt, pre, ot, mt,
    h_send, h_recv, c_send, c_recv, p_send, p_recv,
):
    width, nd = feats_ref.shape
    edges = src_ref.shape[1]
    halo = send_ref.shape[1]
    cdev = cout_ref.shape[0]
    chalo = csend_ref.shape[1]
    mx, my = lax.axis_index("px"), lax.axis_index("py")

    barrier = pltpu.get_barrier_semaphore()
    for k in range(1, n_py):
        pl.semaphore_signal(
            barrier, inc=1, device_id=(mx, lax.rem(my + k, n_py)), device_id_type=MESH
        )

    @pl.when(mx > 0)
    def _():
        pl.semaphore_signal(barrier, inc=1, device_id=(mx - 1, my), device_id_type=MESH)

    @pl.when(mx < n_px - 1)
    def _():
        pl.semaphore_signal(barrier, inc=1, device_id=(mx + 1, my), device_id_type=MESH)

    arrives = (mx > 0, mx < n_px - 1, my > 0, my < n_py - 1)
    leaves = (mx < n_px - 1, mx > 0, my < n_py - 1, my > 0)
    goes_to = (
        (lax.rem(mx + 1, n_px), my),
        (lax.rem(mx + n_px - 1, n_px), my),
        (mx, lax.rem(my + 1, n_py)),
        (mx, lax.rem(my + n_py - 1, n_py)),
    )

    def halo_copy(slot, out, into, amount, send_sem, recv_sem):
        return pltpu.make_async_remote_copy(
            src_ref=out,
            dst_ref=into.at[pl.ds(slot * amount, amount)],
            send_sem=send_sem.at[slot],
            recv_sem=recv_sem.at[slot],
            device_id=goes_to[slot],
            device_id_type=MESH,
        )

    def halo_start(*where):
        for slot in range(4):
            @pl.when(leaves[slot])
            def _():
                halo_copy(slot, *where).start()

    def halo_zero(into, amount):
        for slot in range(4):
            @pl.when(jnp.logical_not(arrives[slot]))
            def _():
                into[slot * amount:(slot + 1) * amount, :] = jnp.zeros((amount, width), BF)

    def halo_arrived(*where):
        for slot in range(4):
            @pl.when(arrives[slot])
            def _():
                halo_copy(slot, *where).wait_recv()

    def halo_sent(*where):
        for slot in range(4):
            @pl.when(leaves[slot])
            def _():
                halo_copy(slot, *where).wait_send()

    feats = feats_ref[...]
    halo_out[...] = dot(feats, one_hot_columns(send_ref[...], 0, nd)).T.astype(BF)

    beside = jnp.where(mx > 0, 1, 0) + jnp.where(mx < n_px - 1, 1, 0)
    pl.semaphore_wait(barrier, n_py - 1 + beside)

    fine = (halo_out, halo_in, halo, h_send, h_recv)
    halo_start(*fine)
    halo_zero(halo_in, halo)
    halo_zero(chalo_in, chalo)

    at_own[...] = dot(ew_ref[:, :width], feats).astype(BF)
    bt[...] = (dot(ew_ref[:, width:], feats) + column(eb_ref)).astype(BF)
    aug[width:, :] = jnp.ones((aug.shape[0] - width, nd), BF)

    def first(step, carry):
        lanes = pl.ds(pl.multiple_of(step * chunk, chunk), chunk)
        target_hot = one_hot_columns(tgt_ref[:, lanes], 0, nd)
        ot[:, lanes] = target_hot
        source_hot = one_hot_columns(src_ref[:, lanes], 0, nd)
        pre[:, lanes] = dot(bt[...], target_hot) + dot(at_own[...], source_hot)
        return carry

    lax.fori_loop(0, edges // chunk, first, 0)

    halo_arrived(*fine)
    at_halo = dot_nt(ew_ref[:, :width], halo_in[...]).astype(BF)
    eo_t = flip(eo_ref)

    def second(step, carry):
        lanes = pl.ds(pl.multiple_of(step * chunk, chunk), chunk)
        source_hot = one_hot_columns(src_ref[:, lanes], nd, 4 * halo)
        hidden = silu(pre[:, lanes] + dot(at_halo, source_hot)).astype(BF)
        mt[:, lanes] = normed(dot(eo_t, hidden), 0).astype(BF)
        return carry

    lax.fori_loop(0, edges // chunk, second, 0)

    incoming = dot_nt(ot[...], mt[...]).T.astype(BF)
    updated = node_part(feats, incoming, nw_ref, nb_ref, no_ref)
    out_ref[...] = updated
    aug[:width, :] = updated

    cluster = owner_ref[...] * cdev + member_ref[...]
    partial = dot_nt(one_hot_columns(cluster, 0, n_py * cdev), aug[...]).astype(BF)
    for k in range(n_py):
        pool_out[k] = partial[k * cdev:(k + 1) * cdev]

    def pool_copy(k):
        peer = lax.rem(my + k, n_py)
        return pltpu.make_async_remote_copy(
            src_ref=pool_out.at[peer],
            dst_ref=pool_in.at[k - 1],
            send_sem=p_send.at[k - 1],
            recv_sem=p_recv.at[k - 1],
            device_id=(mx, peer),
            device_id_type=MESH,
        )

    for k in range(1, n_py):
        pool_copy(k).start()

    ct_hot = one_hot_columns(ctgt_ref[...], 0, cdev)
    cs_hot = one_hot_columns(csrc_ref[...], 0, cdev)
    ch_hot = one_hot_columns(csrc_ref[...], cdev, 4 * chalo)
    ceo_t = flip(ceo_ref)
    total = pool_out[my].astype(F32)
    halo_sent(*fine)

    for k in range(1, n_py):
        pool_copy(k).wait_recv()
        total = total + pool_in[k - 1].astype(F32)
    mean = total[:, :width] / jnp.maximum(total[:, width:width + 1], 1.0)
    coarse = mean.T.astype(BF)

    chalo_out[...] = dot(coarse, one_hot_columns(csend_ref[...], 0, cdev)).T.astype(BF)
    rough = (chalo_out, chalo_in, chalo, c_send, c_recv)
    halo_start(*rough)
    cat = dot(cew_ref[:, :width], coarse).astype(BF)
    cbt = (dot(cew_ref[:, width:], coarse) + column(ceb_ref)).astype(BF)
    cpre = dot(cbt, ct_hot) + dot(cat, cs_hot)
    for k in range(1, n_py):
        pool_copy(k).wait_send()
    halo_arrived(*rough)

    cah = dot_nt(cew_ref[:, :width], chalo_in[...]).astype(BF)
    chidden = silu(cpre + dot(cah, ch_hot)).astype(BF)
    cmt = normed(dot(ceo_t, chidden), 0).astype(BF)
    cincoming = dot_nt(ct_hot, cmt).T.astype(BF)
    cout_ref[...] = node_part(coarse, cincoming, cnw_ref, cnb_ref, cno_ref).astype(F32).T.astype(BF)
    halo_sent(*rough)


def body(n_px, n_py, *args):
    (node_features, edge_source, edge_target, halo_send, edge_weight_in, edge_bias,
     edge_weight_out, node_weight_in, node_bias, node_weight_out, cluster_owner, cluster_member,
     coarse_send, coarse_source, coarse_target, coarse_edge_in, coarse_edge_bias,
     coarse_edge_out, coarse_node_in, coarse_node_bias, coarse_node_out) = args
    nd, width = node_features.shape
    edges, halo, chalo = edge_source.shape[1], halo_send.shape[1], coarse_send.shape[1]
    wide = (width // 128 + 1) * 128
    chunk = math.gcd(edges, 512)
    row = lambda v: v.reshape(1, -1)
    ins = (
        node_features.T, edge_source, edge_target, halo_send, edge_weight_in.T, row(edge_bias),
        edge_weight_out, node_weight_in.T, row(node_bias), node_weight_out, row(cluster_owner),
        row(cluster_member), coarse_send, coarse_source, coarse_target, coarse_edge_in.T,
        row(coarse_edge_bias), coarse_edge_out, coarse_node_in.T, row(coarse_node_bias),
        coarse_node_out,
    )
    vmem = pl.BlockSpec(memory_space=pltpu.VMEM)
    fine, rough = pl.pallas_call(
        functools.partial(kernel, n_px, n_py, chunk),
        out_shape=(
            jax.ShapeDtypeStruct((width, nd), BF),
            jax.ShapeDtypeStruct((CLUST_DEV, width), BF),
        ),
        in_specs=[vmem] * len(ins),
        out_specs=(vmem, vmem),
        scratch_shapes=[
            pltpu.VMEM((halo, width), BF),
            pltpu.VMEM((4 * halo, width), BF),
            pltpu.VMEM((chalo, width), BF),
            pltpu.VMEM((4 * chalo, width), BF),
            pltpu.VMEM((n_py, CLUST_DEV, wide), BF),
            pltpu.VMEM((n_py - 1, CLUST_DEV, wide), BF),
            pltpu.VMEM((wide, nd), BF),
            pltpu.VMEM((width, nd), BF),
            pltpu.VMEM((width, nd), BF),
            pltpu.VMEM((width, edges), F32),
            pltpu.VMEM((nd, edges), BF),
            pltpu.VMEM((width, edges), BF),
            pltpu.SemaphoreType.DMA((4,)),
            pltpu.SemaphoreType.DMA((4,)),
            pltpu.SemaphoreType.DMA((4,)),
            pltpu.SemaphoreType.DMA((4,)),
            pltpu.SemaphoreType.DMA((n_py - 1,)),
            pltpu.SemaphoreType.DMA((n_py - 1,)),
        ],
        compiler_params=pltpu.CompilerParams(
            collective_id=0, has_side_effects=True, vmem_limit_bytes=40 * 1024 * 1024
        ),
    )(*ins)
    return fine.T, rough


def solution(mesh):
    split = P(("px", "py"), None)
    full = P()
    placed = (
        split, split, split, split, full, full, full, full, full, full,
        split, P(("px", "py")), split, split, split, full, full, full, full, full, full,
    )
    return jax.shard_map(
        functools.partial(body, mesh.shape["px"], mesh.shape["py"]),
        mesh=mesh,
        in_specs=placed,
        out_specs=(split, split),
        check_vma=False,
    )
```

```python
import functools
import math

import jax
import jax.numpy as jnp
from jax import lax
from jax.experimental import pallas as pl
from jax.experimental.pallas import tpu as pltpu
from jax.sharding import PartitionSpec as P

CLUST_DEV = 64
BF = jnp.bfloat16
F32 = jnp.float32
MESH = pl.DeviceIdType.MESH


def dot(a, b):
    return jnp.dot(a, b, preferred_element_type=F32)


def dot_nt(a, b):
    return lax.dot_general(a, b, (((1,), (1,)), ((), ())), preferred_element_type=F32)


def silu(x):
    half = 0.5 * x
    return half + half * jnp.tanh(half)


def normed(v, axis):
    scale = 1.0 / v.shape[axis]
    center = v - jnp.sum(v, axis=axis, keepdims=True) * scale
    var = jnp.sum(center * center, axis=axis, keepdims=True) * scale
    return center * lax.rsqrt(var + 1e-05)


def one_hot_columns(ids, first, count):
    rows = lax.broadcasted_iota(jnp.int32, (count, ids.shape[1]), 0)
    return jnp.where(rows == ids - first, 1.0, 0.0).astype(BF)


def column(ref):
    return jnp.broadcast_to(ref[...], (8, ref.shape[1])).T[:, :1]


def flip(ref):
    return ref[...].astype(F32).T.astype(BF)


def node_part(feats, incoming, in_ref, bias_ref, out_ref):
    joined = jnp.concatenate([feats, incoming], axis=0)
    hidden = silu(dot(in_ref[...], joined) + column(bias_ref)).astype(BF)
    return (feats.astype(F32) + normed(dot(flip(out_ref), hidden), 0)).astype(BF)


def kernel(n_px, n_py, chunk, *refs):
    (
        given, outs, (out_ref, cout_ref), held,
        (halo_out, halo_in, chalo_out, chalo_in, pool_out, pool_in, aug),
        (at_own, bt, pre, ot),
        (in_sem, out_sem, h_send, h_recv, c_send, c_recv, p_send, p_recv),
    ) = (refs[:21], refs[21:23], refs[23:25], refs[25:46], refs[46:53], refs[53:57], refs[57:])
    (
        feats_ref, src_ref, tgt_ref, send_ref, ew_ref, eb_ref, eo_ref, nw_ref, nb_ref, no_ref,
        owner_ref, member_ref, csend_ref, csrc_ref, ctgt_ref, cew_ref, ceb_ref, ceo_ref,
        cnw_ref, cnb_ref, cno_ref,
    ) = held

    def load(k):
        return pltpu.make_async_copy(given[k], held[k], in_sem.at[k])

    def loaded(*which):
        for k in which:
            load(k).wait()

    early = (0, 3, 4, 5, 2, 1)
    for k in early:
        load(k).start()

    width, nd = feats_ref.shape
    edges = src_ref.shape[1]
    halo = send_ref.shape[1]
    cdev = cout_ref.shape[0]
    chalo = csend_ref.shape[1]
    mx, my = lax.axis_index("px"), lax.axis_index("py")

    barrier = pltpu.get_barrier_semaphore()
    for k in range(1, n_py):
        pl.semaphore_signal(
            barrier, inc=1, device_id=(mx, lax.rem(my + k, n_py)), device_id_type=MESH
        )

    @pl.when(mx > 0)
    def _():
        pl.semaphore_signal(barrier, inc=1, device_id=(mx - 1, my), device_id_type=MESH)

    @pl.when(mx < n_px - 1)
    def _():
        pl.semaphore_signal(barrier, inc=1, device_id=(mx + 1, my), device_id_type=MESH)

    for k in range(21):
        if k not in early:
            load(k).start()

    arrives = (mx > 0, mx < n_px - 1, my > 0, my < n_py - 1)
    leaves = (mx < n_px - 1, mx > 0, my < n_py - 1, my > 0)
    goes_to = (
        (lax.rem(mx + 1, n_px), my),
        (lax.rem(mx + n_px - 1, n_px), my),
        (mx, lax.rem(my + 1, n_py)),
        (mx, lax.rem(my + n_py - 1, n_py)),
    )

    def halo_copy(slot, out, into, amount, send_sem, recv_sem):
        return pltpu.make_async_remote_copy(
            src_ref=out,
            dst_ref=into.at[pl.ds(slot * amount, amount)],
            send_sem=send_sem.at[slot],
            recv_sem=recv_sem.at[slot],
            device_id=goes_to[slot],
            device_id_type=MESH,
        )

    def halo_start(*where):
        for slot in range(4):
            @pl.when(leaves[slot])
            def _():
                halo_copy(slot, *where).start()

    def halo_zero(into, amount):
        for slot in range(4):
            @pl.when(jnp.logical_not(arrives[slot]))
            def _():
                into[slot * amount:(slot + 1) * amount, :] = jnp.zeros((amount, width), BF)

    def halo_arrived(*where):
        for slot in range(4):
            @pl.when(arrives[slot])
            def _():
                halo_copy(slot, *where).wait_recv()

    def halo_sent(*where):
        for slot in range(4):
            @pl.when(leaves[slot])
            def _():
                halo_copy(slot, *where).wait_send()

    loaded(0, 3)
    feats = feats_ref[...]
    halo_out[...] = dot(feats, one_hot_columns(send_ref[...], 0, nd)).T.astype(BF)

    beside = jnp.where(mx > 0, 1, 0) + jnp.where(mx < n_px - 1, 1, 0)
    pl.semaphore_wait(barrier, n_py - 1 + beside)

    fine = (halo_out, halo_in, halo, h_send, h_recv)
    halo_start(*fine)
    halo_zero(halo_in, halo)
    halo_zero(chalo_in, chalo)

    loaded(4, 5)
    at_own[...] = dot(ew_ref[:, :width], feats).astype(BF)
    bt[...] = (dot(ew_ref[:, width:], feats) + column(eb_ref)).astype(BF)
    aug[width:, :] = jnp.ones((aug.shape[0] - width, nd), BF)

    loaded(2, 1)
    for at in range(0, edges, chunk):
        target_hot = one_hot_columns(tgt_ref[:, at:at + chunk], 0, nd)
        ot[:, at:at + chunk] = target_hot
        source_hot = one_hot_columns(src_ref[:, at:at + chunk], 0, nd)
        pre[:, at:at + chunk] = dot(bt[...], target_hot) + dot(at_own[...], source_hot)

    loaded(*range(6, 21))
    eo_t = flip(eo_ref)
    halo_arrived(*fine)
    at_halo = dot_nt(ew_ref[:, :width], halo_in[...]).astype(BF)

    totals = jnp.zeros((nd, width), F32)
    for at in range(0, edges, chunk):
        source_hot = one_hot_columns(src_ref[:, at:at + chunk], nd, 4 * halo)
        hidden = silu(pre[:, at:at + chunk] + dot(at_halo, source_hot)).astype(BF)
        message = normed(dot(eo_t, hidden), 0).astype(BF)
        totals = totals + dot_nt(ot[:, at:at + chunk], message)

    incoming = totals.T.astype(BF)
    updated = node_part(feats, incoming, nw_ref, nb_ref, no_ref)
    out_ref[...] = updated
    aug[:width, :] = updated
    stores = [
        pltpu.make_async_copy(made, to, out_sem.at[k])
        for k, (made, to) in enumerate(zip((out_ref, cout_ref), outs))
    ]
    stores[0].start()

    cluster = owner_ref[...] * cdev + member_ref[...]
    partial = dot_nt(one_hot_columns(cluster, 0, n_py * cdev), aug[...]).astype(BF)
    for k in range(n_py):
        pool_out[k] = partial[k * cdev:(k + 1) * cdev]

    def pool_copy(k):
        peer = lax.rem(my + k, n_py)
        return pltpu.make_async_remote_copy(
            src_ref=pool_out.at[peer],
            dst_ref=pool_in.at[k - 1],
            send_sem=p_send.at[k - 1],
            recv_sem=p_recv.at[k - 1],
            device_id=(mx, peer),
            device_id_type=MESH,
        )

    for k in range(1, n_py):
        pool_copy(k).start()

    ct_hot = one_hot_columns(ctgt_ref[...], 0, cdev)
    cs_hot = one_hot_columns(csrc_ref[...], 0, cdev)
    ch_hot = one_hot_columns(csrc_ref[...], cdev, 4 * chalo)
    ceo_t = flip(ceo_ref)
    total = pool_out[my].astype(F32)
    halo_sent(*fine)

    for k in range(1, n_py):
        pool_copy(k).wait_recv()
        total = total + pool_in[k - 1].astype(F32)
    mean = total[:, :width] / jnp.maximum(total[:, width:width + 1], 1.0)
    coarse = mean.T.astype(BF)

    chalo_out[...] = dot(coarse, one_hot_columns(csend_ref[...], 0, cdev)).T.astype(BF)
    rough = (chalo_out, chalo_in, chalo, c_send, c_recv)
    halo_start(*rough)
    cat = dot(cew_ref[:, :width], coarse).astype(BF)
    cbt = (dot(cew_ref[:, width:], coarse) + column(ceb_ref)).astype(BF)
    cpre = dot(cbt, ct_hot) + dot(cat, cs_hot)
    for k in range(1, n_py):
        pool_copy(k).wait_send()
    halo_arrived(*rough)

    cah = dot_nt(cew_ref[:, :width], chalo_in[...]).astype(BF)
    chidden = silu(cpre + dot(cah, ch_hot)).astype(BF)
    cmt = normed(dot(ceo_t, chidden), 0).astype(BF)
    cincoming = dot_nt(ct_hot, cmt).T.astype(BF)
    cout_ref[...] = node_part(coarse, cincoming, cnw_ref, cnb_ref, cno_ref).astype(F32).T.astype(BF)
    stores[1].start()
    halo_sent(*rough)
    for store in stores:
        store.wait()


def body(n_px, n_py, *args):
    (node_features, edge_source, edge_target, halo_send, edge_weight_in, edge_bias,
     edge_weight_out, node_weight_in, node_bias, node_weight_out, cluster_owner, cluster_member,
     coarse_send, coarse_source, coarse_target, coarse_edge_in, coarse_edge_bias,
     coarse_edge_out, coarse_node_in, coarse_node_bias, coarse_node_out) = args
    nd, width = node_features.shape
    edges, halo, chalo = edge_source.shape[1], halo_send.shape[1], coarse_send.shape[1]
    wide = (width // 128 + 1) * 128
    chunk = math.gcd(edges, 512)
    row = lambda v: v.reshape(1, -1)
    ins = (
        node_features.T, edge_source, edge_target, halo_send, edge_weight_in.T, row(edge_bias),
        edge_weight_out, node_weight_in.T, row(node_bias), node_weight_out, row(cluster_owner),
        row(cluster_member), coarse_send, coarse_source, coarse_target, coarse_edge_in.T,
        row(coarse_edge_bias), coarse_edge_out, coarse_node_in.T, row(coarse_node_bias),
        coarse_node_out,
    )
    hbm = pl.BlockSpec(memory_space=pltpu.HBM)
    fine, rough = pl.pallas_call(
        functools.partial(kernel, n_px, n_py, chunk),
        out_shape=(
            jax.ShapeDtypeStruct((width, nd), BF),
            jax.ShapeDtypeStruct((CLUST_DEV, width), BF),
        ),
        in_specs=[hbm] * len(ins),
        out_specs=(hbm, hbm),
        scratch_shapes=[pltpu.VMEM((width, nd), BF), pltpu.VMEM((CLUST_DEV, width), BF)]
        + [pltpu.VMEM(v.shape, v.dtype) for v in ins] + [
            pltpu.VMEM((halo, width), BF),
            pltpu.VMEM((4 * halo, width), BF),
            pltpu.VMEM((chalo, width), BF),
            pltpu.VMEM((4 * chalo, width), BF),
            pltpu.VMEM((n_py, CLUST_DEV, wide), BF),
            pltpu.VMEM((n_py - 1, CLUST_DEV, wide), BF),
            pltpu.VMEM((wide, nd), BF),
            pltpu.VMEM((width, nd), BF),
            pltpu.VMEM((width, nd), BF),
            pltpu.VMEM((width, edges), F32),
            pltpu.VMEM((nd, edges), BF),
            pltpu.SemaphoreType.DMA((len(ins),)),
            pltpu.SemaphoreType.DMA((2,)),
            pltpu.SemaphoreType.DMA((4,)),
            pltpu.SemaphoreType.DMA((4,)),
            pltpu.SemaphoreType.DMA((4,)),
            pltpu.SemaphoreType.DMA((4,)),
            pltpu.SemaphoreType.DMA((n_py - 1,)),
            pltpu.SemaphoreType.DMA((n_py - 1,)),
        ],
        compiler_params=pltpu.CompilerParams(
            collective_id=0, has_side_effects=True, vmem_limit_bytes=64 * 1024 * 1024
        ),
    )(*ins)
    return fine.T, rough


def solution(mesh):
    split = P(("px", "py"), None)
    full = P()
    placed = (
        split, split, split, split, full, full, full, full, full, full,
        split, P(("px", "py")), split, split, split, full, full, full, full, full, full,
    )
    return jax.shard_map(
        functools.partial(body, mesh.shape["px"], mesh.shape["py"]),
        mesh=mesh,
        in_specs=placed,
        out_specs=(split, split),
        check_vma=False,
    )
```

```python
import functools
import math

import jax
import jax.numpy as jnp
from jax import lax
from jax.experimental import pallas as pl
from jax.experimental.pallas import tpu as pltpu
from jax.sharding import PartitionSpec as P

CLUST_DEV = 64
BF = jnp.bfloat16
F32 = jnp.float32
MESH = pl.DeviceIdType.MESH


def dot(a, b):
    return jnp.dot(a, b, preferred_element_type=F32)


def dot_nt(a, b):
    return lax.dot_general(a, b, (((1,), (1,)), ((), ())), preferred_element_type=F32)


def silu(x):
    half = 0.5 * x
    return half + half * jnp.tanh(half)


def normed(v, axis):
    scale = 1.0 / v.shape[axis]
    center = v - jnp.sum(v, axis=axis, keepdims=True) * scale
    var = jnp.sum(center * center, axis=axis, keepdims=True) * scale
    return center * lax.rsqrt(var + 1e-05)


def one_hot_columns(ids, first, count):
    shape = (count, ids.shape[1])
    rows = lax.broadcasted_iota(jnp.int16, shape, 0)
    wanted = jnp.broadcast_to((ids - first).astype(jnp.int16), shape)
    return jnp.where(rows == wanted, jnp.ones(shape, BF), jnp.zeros(shape, BF))


def column(ref):
    return jnp.broadcast_to(ref[...], (8, ref.shape[1])).T[:, :1]


def flip(ref):
    return ref[...].astype(F32).T.astype(BF)


def node_part(feats, incoming, in_ref, bias_ref, out_ref):
    joined = jnp.concatenate([feats, incoming], axis=0)
    hidden = silu(dot(in_ref[...], joined) + column(bias_ref)).astype(BF)
    return (feats.astype(F32) + normed(dot(flip(out_ref), hidden), 0)).astype(BF)


def kernel(n_px, n_py, chunk, *refs):
    (
        given, outs, (out_ref, cout_ref), held,
        (halo_out, halo_in, chalo_out, chalo_in, pool_out, pool_in, aug),
        (at_own, bt, pre, ot),
        (in_sem, out_sem, h_send, h_recv, c_send, c_recv, p_send, p_recv),
    ) = (refs[:21], refs[21:23], refs[23:25], refs[25:46], refs[46:53], refs[53:57], refs[57:])
    (
        feats_ref, src_ref, tgt_ref, send_ref, ew_ref, eb_ref, eo_ref, nw_ref, nb_ref, no_ref,
        owner_ref, member_ref, csend_ref, csrc_ref, ctgt_ref, cew_ref, ceb_ref, ceo_ref,
        cnw_ref, cnb_ref, cno_ref,
    ) = held

    def load(k):
        return pltpu.make_async_copy(given[k], held[k], in_sem.at[k])

    def loaded(*which):
        for k in which:
            load(k).wait()

    early = (0, 3, 4, 5, 2, 1)
    for k in early:
        load(k).start()

    width, nd = feats_ref.shape
    edges = src_ref.shape[1]
    halo = send_ref.shape[1]
    cdev = cout_ref.shape[0]
    chalo = csend_ref.shape[1]
    mx, my = lax.axis_index("px"), lax.axis_index("py")

    barrier = pltpu.get_barrier_semaphore()
    for k in range(1, n_py):
        pl.semaphore_signal(
            barrier, inc=1, device_id=(mx, lax.rem(my + k, n_py)), device_id_type=MESH
        )

    @pl.when(mx > 0)
    def _():
        pl.semaphore_signal(barrier, inc=1, device_id=(mx - 1, my), device_id_type=MESH)

    @pl.when(mx < n_px - 1)
    def _():
        pl.semaphore_signal(barrier, inc=1, device_id=(mx + 1, my), device_id_type=MESH)

    for k in range(21):
        if k not in early:
            load(k).start()

    arrives = (mx > 0, mx < n_px - 1, my > 0, my < n_py - 1)
    leaves = (mx < n_px - 1, mx > 0, my < n_py - 1, my > 0)
    goes_to = (
        (lax.rem(mx + 1, n_px), my),
        (lax.rem(mx + n_px - 1, n_px), my),
        (mx, lax.rem(my + 1, n_py)),
        (mx, lax.rem(my + n_py - 1, n_py)),
    )

    def halo_copy(slot, out, into, amount, send_sem, recv_sem):
        return pltpu.make_async_remote_copy(
            src_ref=out,
            dst_ref=into.at[pl.ds(slot * amount, amount)],
            send_sem=send_sem.at[slot],
            recv_sem=recv_sem.at[slot],
            device_id=goes_to[slot],
            device_id_type=MESH,
        )

    def halo_start(*where):
        for slot in range(4):
            @pl.when(leaves[slot])
            def _():
                halo_copy(slot, *where).start()

    def halo_zero(into, amount):
        for slot in range(4):
            @pl.when(jnp.logical_not(arrives[slot]))
            def _():
                into[slot * amount:(slot + 1) * amount, :] = jnp.zeros((amount, width), BF)

    def halo_arrived(*where):
        for slot in range(4):
            @pl.when(arrives[slot])
            def _():
                halo_copy(slot, *where).wait_recv()

    def halo_sent(*where):
        for slot in range(4):
            @pl.when(leaves[slot])
            def _():
                halo_copy(slot, *where).wait_send()

    loaded(0, 3)
    feats = feats_ref[...]
    halo_out[...] = dot(feats, one_hot_columns(send_ref[...], 0, nd)).T.astype(BF)

    beside = jnp.where(mx > 0, 1, 0) + jnp.where(mx < n_px - 1, 1, 0)
    pl.semaphore_wait(barrier, n_py - 1 + beside)

    fine = (halo_out, halo_in, halo, h_send, h_recv)
    halo_start(*fine)
    halo_zero(halo_in, halo)
    halo_zero(chalo_in, chalo)

    loaded(4, 5)
    at_own[...] = dot(ew_ref[:, :width], feats).astype(BF)
    bt[...] = (dot(ew_ref[:, width:], feats) + column(eb_ref)).astype(BF)
    aug[width:, :] = jnp.ones((aug.shape[0] - width, nd), BF)

    loaded(2, 1)
    for at in range(0, edges, chunk):
        target_hot = one_hot_columns(tgt_ref[:, at:at + chunk], 0, nd)
        ot[:, at:at + chunk] = target_hot
        source_hot = one_hot_columns(src_ref[:, at:at + chunk], 0, nd)
        pre[:, at:at + chunk] = dot(bt[...], target_hot) + dot(at_own[...], source_hot)

    loaded(*range(6, 21))
    eo_t = flip(eo_ref)
    halo_arrived(*fine)
    at_halo = dot_nt(ew_ref[:, :width], halo_in[...]).astype(BF)

    totals = jnp.zeros((nd, width), F32)
    for at in range(0, edges, chunk):
        source_hot = one_hot_columns(src_ref[:, at:at + chunk], nd, 4 * halo)
        hidden = silu(pre[:, at:at + chunk] + dot(at_halo, source_hot)).astype(BF)
        message = normed(dot(eo_t, hidden), 0).astype(BF)
        totals = totals + dot_nt(ot[:, at:at + chunk], message)

    incoming = totals.T.astype(BF)
    updated = node_part(feats, incoming, nw_ref, nb_ref, no_ref)
    out_ref[...] = updated
    aug[:width, :] = updated
    stores = [
        pltpu.make_async_copy(made, to, out_sem.at[k])
        for k, (made, to) in enumerate(zip((out_ref, cout_ref), outs))
    ]
    stores[0].start()

    cluster = owner_ref[...] * cdev + member_ref[...]
    partial = dot_nt(one_hot_columns(cluster, 0, n_py * cdev), aug[...]).astype(BF)
    for k in range(n_py):
        pool_out[k] = partial[k * cdev:(k + 1) * cdev]

    def pool_copy(k):
        peer = lax.rem(my + k, n_py)
        return pltpu.make_async_remote_copy(
            src_ref=pool_out.at[peer],
            dst_ref=pool_in.at[k - 1],
            send_sem=p_send.at[k - 1],
            recv_sem=p_recv.at[k - 1],
            device_id=(mx, peer),
            device_id_type=MESH,
        )

    for k in range(1, n_py):
        pool_copy(k).start()

    ct_hot = one_hot_columns(ctgt_ref[...], 0, cdev)
    cs_hot = one_hot_columns(csrc_ref[...], 0, cdev)
    ch_hot = one_hot_columns(csrc_ref[...], cdev, 4 * chalo)
    ceo_t = flip(ceo_ref)
    total = pool_out[my].astype(F32)
    halo_sent(*fine)

    for k in range(1, n_py):
        pool_copy(k).wait_recv()
        total = total + pool_in[k - 1].astype(F32)
    mean = total[:, :width] / jnp.maximum(total[:, width:width + 1], 1.0)
    coarse = mean.T.astype(BF)

    chalo_out[...] = dot(coarse, one_hot_columns(csend_ref[...], 0, cdev)).T.astype(BF)
    rough = (chalo_out, chalo_in, chalo, c_send, c_recv)
    halo_start(*rough)
    cat = dot(cew_ref[:, :width], coarse).astype(BF)
    cbt = (dot(cew_ref[:, width:], coarse) + column(ceb_ref)).astype(BF)
    cpre = dot(cbt, ct_hot) + dot(cat, cs_hot)
    for k in range(1, n_py):
        pool_copy(k).wait_send()
    halo_arrived(*rough)

    cah = dot_nt(cew_ref[:, :width], chalo_in[...]).astype(BF)
    chidden = silu(cpre + dot(cah, ch_hot)).astype(BF)
    cmt = normed(dot(ceo_t, chidden), 0).astype(BF)
    cincoming = dot_nt(ct_hot, cmt).T.astype(BF)
    cout_ref[...] = node_part(coarse, cincoming, cnw_ref, cnb_ref, cno_ref).astype(F32).T.astype(BF)
    stores[1].start()
    halo_sent(*rough)
    for store in stores:
        store.wait()


def body(n_px, n_py, *args):
    (node_features, edge_source, edge_target, halo_send, edge_weight_in, edge_bias,
     edge_weight_out, node_weight_in, node_bias, node_weight_out, cluster_owner, cluster_member,
     coarse_send, coarse_source, coarse_target, coarse_edge_in, coarse_edge_bias,
     coarse_edge_out, coarse_node_in, coarse_node_bias, coarse_node_out) = args
    nd, width = node_features.shape
    edges, halo, chalo = edge_source.shape[1], halo_send.shape[1], coarse_send.shape[1]
    wide = (width // 128 + 1) * 128
    chunk = math.gcd(edges, 512)
    row = lambda v: v.reshape(1, -1)
    ins = (
        node_features.T, edge_source, edge_target, halo_send, edge_weight_in.T, row(edge_bias),
        edge_weight_out, node_weight_in.T, row(node_bias), node_weight_out, row(cluster_owner),
        row(cluster_member), coarse_send, coarse_source, coarse_target, coarse_edge_in.T,
        row(coarse_edge_bias), coarse_edge_out, coarse_node_in.T, row(coarse_node_bias),
        coarse_node_out,
    )
    hbm = pl.BlockSpec(memory_space=pltpu.HBM)
    fine, rough = pl.pallas_call(
        functools.partial(kernel, n_px, n_py, chunk),
        out_shape=(
            pltpu.VMEM((width, nd), BF),
            pltpu.VMEM((CLUST_DEV, width), BF),
        ),
        in_specs=[hbm] * len(ins),
        out_specs=(pl.BlockSpec(memory_space=pltpu.VMEM),) * 2,
        scratch_shapes=[pltpu.VMEM((width, nd), BF), pltpu.VMEM((CLUST_DEV, width), BF)]
        + [pltpu.VMEM(v.shape, v.dtype) for v in ins] + [
            pltpu.VMEM((halo, width), BF),
            pltpu.VMEM((4 * halo, width), BF),
            pltpu.VMEM((chalo, width), BF),
            pltpu.VMEM((4 * chalo, width), BF),
            pltpu.VMEM((n_py, CLUST_DEV, wide), BF),
            pltpu.VMEM((n_py - 1, CLUST_DEV, wide), BF),
            pltpu.VMEM((wide, nd), BF),
            pltpu.VMEM((width, nd), BF),
            pltpu.VMEM((width, nd), BF),
            pltpu.VMEM((width, edges), F32),
            pltpu.VMEM((nd, edges), BF),
            pltpu.SemaphoreType.DMA((len(ins),)),
            pltpu.SemaphoreType.DMA((2,)),
            pltpu.SemaphoreType.DMA((4,)),
            pltpu.SemaphoreType.DMA((4,)),
            pltpu.SemaphoreType.DMA((4,)),
            pltpu.SemaphoreType.DMA((4,)),
            pltpu.SemaphoreType.DMA((n_py - 1,)),
            pltpu.SemaphoreType.DMA((n_py - 1,)),
        ],
        compiler_params=pltpu.CompilerParams(
            collective_id=0, has_side_effects=True, vmem_limit_bytes=64 * 1024 * 1024 - 512 * 1024
        ),
    )(*ins)
    return fine.T, rough


def solution(mesh):
    split = P(("px", "py"), None)
    full = P()
    placed = (
        split, split, split, split, full, full, full, full, full, full,
        split, P(("px", "py")), split, split, split, full, full, full, full, full, full,
    )
    return jax.shard_map(
        functools.partial(body, mesh.shape["px"], mesh.shape["py"]),
        mesh=mesh,
        in_specs=placed,
        out_specs=(split, split),
        check_vma=False,
    )
```
